256 devices in a mesh: row: 8 (over y, core), col: 32 (over z, x).
Axes of the slice: x: 4, y: 4, z: 8, core: 2. Of those that a mesh axis runs over, the one named last changes fastest.
Arguments:
- tokens: bfloat16 [512, 12288], P('col', 'row'), may hold values from -6 to 6
- grad_out: bfloat16 [512, 12288], P('col', 'row'), may hold values from -6 to 6
- w_in: bfloat16 [12288, 24576], P('row', 'col'), may hold values from -0.0546875 to 0.0546875
- w_out: bfloat16 [24576, 12288], P('col', 'row'), may hold values from -0.0390625 to 0.0390625
Outputs:
- grad_in: bfloat16 [512, 12288], P('col', 'row')
- grad_w_in: bfloat16 [12288, 24576], P('row', 'col')
- grad_w_out: bfloat16 [24576, 12288], P('col', 'row')
The draws below stay inside these ranges and needn't reach their ends.
All inputs are finite; a program needn't handle non-finite values.
Results may differ from the reference program's by a relative error of at most 0.022.
Values may be sent and summed in bfloat16 or wider, within the bound.
A program may use at most 64 MiB of HBM per device.

```python
import math
import jax
import jax.numpy as jnp

D = 12288
FF = 24576
TOKENS = 512


def levels(own_key, shape, cuts, low, high):
    loudness, own = 1.0, jax.random.fold_in(own_key, 6)
    for dim, blocks in cuts:
        draws = jnp.exp(jax.random.uniform(jax.random.fold_in(own, dim), (blocks,), jnp.float32, low / len(cuts), high / len(cuts)))
        loudness = loudness * jnp.repeat(draws, shape[dim] // blocks).reshape([-1 if axis == dim else 1 for axis in range(len(shape))])
    return loudness


def centred(rng, shape, width, reach, cuts=(), dtype=jnp.bfloat16):
    entries = jax.random.normal(rng, shape, jnp.float32) * width
    if len(cuts) > 0:
        entries = levels(rng, shape, cuts, -0.22, 0.18) * entries
    return jnp.clip(entries, min=-reach, max=reach).astype(dtype)


def setup_inputs(seed: int = 0) -> dict:
    splits = jax.random.split(jax.random.key(seed), 5)
    return {
        "tokens": centred(splits[0], (TOKENS, D), 1.0, 6.0, ((0, 32), (1, 8))),
        "grad_out": centred(splits[1], (TOKENS, D), 1.0, 6.0, ((0, 32), (1, 8))),
        "w_in": centred(splits[2], (D, FF), D ** -0.5, 0.0546875, ((0, 8), (1, 32))),
        "w_out": centred(splits[3], (FF, D), FF ** -0.5, 0.0390625, ((0, 32), (1, 8))),
    }


def gelu_pair(pre_act, back_act):
    coeff = math.sqrt(2.0 / math.pi)
    inner = coeff * (pre_act + 0.044715 * pre_act * pre_act * pre_act)
    tanh_val = jnp.tanh(inner)
    activated = (0.5 * pre_act * (1.0 + tanh_val)).astype(jnp.bfloat16)
    slope = 0.5 * (1.0 + tanh_val) + 0.5 * pre_act * (1.0 - tanh_val * tanh_val) * coeff * (1.0 + 3.0 * 0.044715 * pre_act * pre_act)
    grad_pre = (back_act * slope).astype(jnp.bfloat16)
    return (activated, grad_pre)

def reference(tokens, grad_out, w_in, w_out):
    pre_act = jnp.dot(tokens, w_in, preferred_element_type=jnp.float32)
    back_act = jnp.dot(grad_out, w_out.T, preferred_element_type=jnp.float32)
    activated, grad_pre = gelu_pair(pre_act, back_act)
    grad_w_out = jnp.dot(activated.T, grad_out, preferred_element_type=jnp.float32).astype(jnp.bfloat16)
    grad_w_in = jnp.dot(tokens.T, grad_pre, preferred_element_type=jnp.float32).astype(jnp.bfloat16)
    grad_in = jnp.dot(grad_pre, w_in.T, preferred_element_type=jnp.float32).astype(jnp.bfloat16)
    return (grad_in, grad_w_in, grad_w_out)
```

```python
import math

import jax
import jax.numpy as jnp
from jax import lax
from jax.experimental import pallas as pl
from jax.experimental.pallas import tpu as pltpu
from jax.sharding import PartitionSpec as P

F32, BF16 = jnp.float32, jnp.bfloat16
MESH = pl.DeviceIdType.MESH
D, FF, TOK = 1536, 768, 512
HALF = FF // 2
ROWS = 16
CA = 640
ZA = 256
ZB = D - ZA
GROUPS = ((0, 4), (4, 8), (12, 8), (20, 8), (28, 4))
XOFF = (0, 1, -1, 2)
ORDER = (
    ('init',), ('ax', 2), ('ax', 1), ('bz', 1, 0), ('bz', 1, 1), ('az', 1, 0, 0), ('az', 1, 1, 0), ('bx', 0, 0, 2),
    ('bx', 0, 0, 1), ('ax', 3), ('az', 1, 0, 2), ('az', 1, 1, 2), ('bx', 1, 0, 2), ('az', 1, 0, 1), ('az', 1, 1, 1),
    ('bx', 1, 0, 1), ('bx', 1, 1, 2), ('bz', 2, 0), ('bx', 1, 1, 1), ('bz', 2, 1), ('S1', 0), ('az', 1, 0, 3),
    ('az', 1, 1, 3), ('az', 2, 0, 0), ('az', 2, 1, 0), ('az', 2, 0, 2), ('az', 2, 1, 2), ('bx', 2, 0, 1),
    ('az', 2, 0, 1), ('az', 2, 1, 1), ('S2', 0), ('bx', 2, 0, 2), ('S1', 1), ('az', 2, 0, 3), ('bx', 2, 1, 1),
    ('bx', 2, 1, 2), ('az', 2, 1, 3), ('bz', 3, 0), ('bz', 3, 1), ('az', 3, 0, 0), ('az', 3, 1, 0), ('az', 3, 0, 2),
    ('az', 3, 1, 2), ('S2', 1), ('S3', 0), ('az', 3, 0, 1), ('az', 3, 1, 1), ('S1', 2), ('bx', 3, 0, 1),
    ('bx', 3, 0, 2), ('az', 3, 0, 3), ('az', 3, 1, 3), ('bz', 4, 0), ('bx', 3, 1, 1), ('bx', 3, 1, 2), ('S2', 2),
    ('S3', 1), ('S4', 0), ('bx', 4, 0, 1), ('bx', 4, 0, 2), ('S5', 0), ('S1', 3), ('S3', 2), ('S1', 4), ('S6', 0),
    ('S4', 1), ('S2', 3), ('S2', 4), ('S5', 1), ('S4', 2), ('S5', 2), ('S3', 3), ('S3', 4), ('S6', 1), ('S4', 3),
    ('S6', 2), ('S4', 4), ('S5', 3), ('S5', 4), ('W', 0), ('W', 1), ('S6', 3), ('E1',), ('S6', 4), ('E3',), ('E2',),
)


def ways(s):
    return (0, 1) if s in (1, 2, 3) else (0,)


def block(s, d, f):
    return GROUPS[s][0] + 4 * d + f


def gelu_pair(pre_act, back_act):
    coeff = math.sqrt(2.0 / math.pi)
    inner = coeff * (pre_act + 0.044715 * pre_act * pre_act * pre_act)
    tanh_val = jnp.tanh(inner)
    activated = (0.5 * pre_act * (1.0 + tanh_val)).astype(BF16)
    slope = 0.5 * (1.0 + tanh_val) + 0.5 * pre_act * (1.0 - tanh_val * tanh_val) * coeff * (
        1.0 + 3.0 * 0.044715 * pre_act * pre_act
    )
    return activated, (back_act * slope).astype(BF16)


def dot(a, b, dims):
    return lax.dot_general(a, b, ((dims[:1], dims[1:]), ((), ())), preferred_element_type=F32)


def kernel(
    tok_hbm, grad_hbm, win_hbm, wout_hbm, GIN, GW1, GW2,
    X, W1, W2, KS, KO, KR, C, R, H, G, RA, SA, RX, RB, SB, RZ, OUT,
    local_sem,
    a_send, a_recv, b_send, b_recv, k_send, k_recv, r_send, r_recv, y_send, y_recv, h_send, h_recv,
    ra_send, ra_recv, rb_send, rb_recv, rx_send, rx_recv, rz_send, rz_recv,
):
    row, col = lax.axis_index("row"), lax.axis_index("col")
    y, core, z, x = row // 2, row % 2, col // 4, col % 4

    def at(dz=0, dx=0, dy=0, other=False):
        return {
            "row": lax.rem(y + dy + 4, 4) * 2 + (1 - core if other else core),
            "col": lax.rem(z + dz + 8, 8) * 4 + lax.rem(x + dx + 4, 4),
        }

    mine = pl.multiple_of(core * HALF, HALF)
    theirs = pl.multiple_of((1 - core) * HALF, HALF)
    local = [
        pltpu.make_async_copy(tok_hbm, X.at[0, pl.ds(0, ROWS)], local_sem.at[0]),
        pltpu.make_async_copy(grad_hbm, X.at[1, pl.ds(0, ROWS)], local_sem.at[1]),
        pltpu.make_async_copy(win_hbm.at[:, pl.ds(mine, HALF)], W1.at[:, pl.ds(0, HALF)], local_sem.at[2]),
        pltpu.make_async_copy(win_hbm.at[:, pl.ds(theirs, HALF)], W1.at[:, pl.ds(HALF, HALF)], local_sem.at[3]),
        pltpu.make_async_copy(wout_hbm.at[pl.ds(mine, HALF)], W2.at[pl.ds(0, HALF)], local_sem.at[4]),
        pltpu.make_async_copy(wout_hbm.at[pl.ds(theirs, HALF)], W2.at[pl.ds(HALF, HALF)], local_sem.at[5]),
    ]
    for copy in local:
        copy.start()

    partners = [at(dz=i) for i in range(1, 8)] + [at(dx=i) for i in range(1, 4)] + [at(dy=i) for i in range(1, 4)]
    partners.append(at(other=True))
    barrier = pltpu.get_barrier_semaphore()
    for partner in partners:
        pl.semaphore_signal(barrier, inc=1, device_id=partner, device_id_type=MESH)
    pl.semaphore_wait(barrier, len(partners))

    unsent = []

    def remote(src, dst, send, recv, target):
        return pltpu.make_async_remote_copy(
            src_ref=src, dst_ref=dst, send_sem=send, recv_sem=recv, device_id=target, device_id_type=MESH
        )

    def start(copy):
        copy.start()
        unsent.append(copy)

    def piece(part, s, d, f, which):
        array = pl.ds(0, 2) if which is None else pl.ds(which, 1)
        columns = pl.ds(0, CA) if part == 0 else pl.ds(CA, D - CA)
        return X.at[array, pl.ds(ROWS * block(s, d, f), ROWS), columns]

    def gather(part, src, dst, target, which=None):
        i = 2 * block(*dst) + (which or 0)
        send, recv = (a_send, a_recv) if part == 0 else (b_send, b_recv)
        return remote(piece(part, *src, which), piece(part, *dst, which), send.at[i], recv.at[i], target)

    def arrived(part, s, d, f, which=None):
        gather(part, (s, d, f), (s, d, f), at(dz=1), which).wait_recv()

    def along_z(part, s, d, f):
        if s == 0:
            start(gather(part, (0, 0, f), (1, 0, f), at(dz=1)))
            start(gather(part, (0, 0, f), (1, 1, f), at(dz=-1)))
        elif s < 3:
            start(gather(part, (s, d, f), (s + 1, d, f), at(dz=-1 if d else 1)))
        elif s == 3:
            start(gather(part, (3, d, f), (4, 0, f), at(dz=-1 if d else 1), d))

    def along_x(part, s, d):
        start(gather(part, (s, d, 0), (s, d, 2), at(dx=1)))
        start(gather(part, (s, d, 0), (s, d, 1), at(dx=-1)))

    def further_x(part, s, d, f):
        start(gather(part, (s, d, f), (s, d, 3), at(dx=-1 if f == 1 else 1), f - 1))

    def begin():
        local[0].wait()
        local[1].wait()
        along_z(1, 0, 0, 0)
        along_x(0, 0, 0)
        along_z(0, 0, 0, 0)
        along_x(1, 0, 0)

    def ax(f):
        if f == 3:
            arrived(0, 0, 0, 3, 0)
            arrived(0, 0, 0, 3, 1)
        else:
            arrived(0, 0, 0, f)
        along_z(0, 0, 0, f)
        if f < 3:
            further_x(0, 0, 0, f)

    def az(s, d, f):
        arrived(0, s, d, f)
        along_z(0, s, d, f)

    def bz(s, d):
        if s == 4:
            arrived(1, 4, 0, 0, 0)
            arrived(1, 4, 0, 0, 1)
        else:
            arrived(1, s, d, 0)
        along_z(1, s, d, 0)
        along_x(1, s, d)

    def bx(s, d, f):
        arrived(1, s, d, f)
        further_x(1, s, d, f)

    def rows(s):
        return ROWS * GROUPS[s][0], ROWS * GROUPS[s][1]

    def swap_copy(s):
        first, n = rows(s)
        part = pl.ds(first, n)
        return remote(KS.at[:, part], KR.at[:, part], k_send.at[s], k_recv.at[s], at(other=True))

    def s1(s):
        for d in ways(s):
            arrived(1, s, d, 3, 0)
            arrived(1, s, d, 3, 1)
        if s == 4:
            for f in range(4):
                arrived(0, 4, 0, f, 0)
                arrived(0, 4, 0, f, 1)
        first, n = rows(s)
        part = pl.ds(first, n)
        if s == 0:
            local[2].wait()
            local[3].wait()
        pre = dot(X[0, part, :], W1[...], (1, 0))
        KO[0, part, :] = pre[:, :HALF]
        KS[0, part, :] = pre[:, HALF:].astype(BF16)
        if s == 0:
            local[4].wait()
            local[5].wait()
        back = dot(X[1, part, :], W2[...], (1, 1))
        KO[1, part, :] = back[:, :HALF]
        KS[1, part, :] = back[:, HALF:].astype(BF16)
        start(swap_copy(s))

    def quarter(s, i):
        first, n = rows(s)
        return pl.ds(pl.multiple_of(first + i * (n // 4), ROWS), n // 4)

    def sum_copy(s, dy):
        n = rows(s)[1] // 4
        there = R.at[dy - 1, :, pl.ds(rows(s)[0] // 4, n)]
        return remote(
            C.at[:, quarter(s, lax.rem(y + dy, 4))], there, r_send.at[s, dy - 1], r_recv.at[s, dy - 1], at(dy=dy)
        )

    def s2(s):
        first, n = rows(s)
        part = pl.ds(first, n)
        swap_copy(s).wait_recv()
        C[:, part, :] = (KO[:, part, :] + KR[:, part, :].astype(F32)).astype(BF16)
        for dy in (2, 1, 3):
            start(sum_copy(s, dy))

    def part_copy(s, dy):
        where = H.at[:, quarter(s, y), pl.ds(0, HALF)]
        return remote(where, where, y_send.at[s, dy - 1], y_recv.at[s, dy - 1], at(dy=dy))

    def s3(s):
        for dy in (1, 2, 3):
            sum_copy(s, dy).wait_recv()
        total = C[:, quarter(s, y), :].astype(F32)
        for i in range(3):
            total += R[i, :, pl.ds(rows(s)[0] // 4, rows(s)[1] // 4), :].astype(F32)
        activated, grad_pre = gelu_pair(total[0], total[1])
        H[0, quarter(s, y), 0:HALF] = activated
        H[1, quarter(s, y), 0:HALF] = grad_pre
        for dy in (2, 1, 3):
            start(part_copy(s, dy))

    def half_copy(s):
        first, n = rows(s)
        part = pl.ds(first, n)
        return remote(
            H.at[:, part, pl.ds(0, HALF)], H.at[:, part, pl.ds(HALF, HALF)], h_send.at[s], h_recv.at[s], at(other=True)
        )

    def s4(s):
        for dy in (1, 2, 3):
            part_copy(s, dy).wait_recv()
        start(half_copy(s))

    def ra_copy(s, d):
        i = 2 * (s - 1) + d
        there = RA.at[i]
        src = G.at[pl.ds(ROWS * block(s, d, 0), 4 * ROWS), pl.ds(0, ZA)]
        return remote(src, there, ra_send.at[i], ra_recv.at[i], at(dz=s if d else -s))

    def rb_copy(s, d, f):
        i, j = 2 * s + d, f - 1
        src = G.at[pl.ds(ROWS * block(s, d, f), ROWS), pl.ds(ZA, ZB)]
        return remote(src, RB.at[i, j], rb_send.at[i, j], rb_recv.at[i, j], at(dx=XOFF[f]))

    def rz_copy(s, d):
        i = 2 * (s - 1) + d
        return remote(SB.at[i], RZ.at[i], rz_send.at[i], rz_recv.at[i], at(dz=s if d else -s))

    def rx_copy(f):
        src = SA.at[pl.ds(ROWS * f, ROWS)]
        return remote(src, RX.at[f - 1], rx_send.at[f - 1], rx_recv.at[f - 1], at(dx=XOFF[f]))

    def s5(s):
        half_copy(s).wait_recv()
        first, n = rows(s)
        part = pl.ds(first, n)
        G[part, :] = dot(H[1, part, :], W1[...], (1, 1)).astype(BF16)
        for d in ways(s):
            if s:
                start(ra_copy(s, d))
            for f in (3, 1, 2):
                start(rb_copy(s, d, f))

    def s6(s):
        for d in ways(s):
            for f in (1, 2, 3):
                rb_copy(s, d, f).wait_recv()
            i = 2 * s + d
            total = G[pl.ds(ROWS * block(s, d, 0), ROWS), pl.ds(ZA, ZB)].astype(F32)
            for j in range(3):
                total += RB[i, j].astype(F32)
            if s:
                SB[2 * (s - 1) + d] = total.astype(BF16)
                start(rz_copy(s, d))
            else:
                OUT[:, pl.ds(ZA, ZB)] = total

    def w(i):
        if i == 0:
            total = dot(X[0], H[1], (0, 0)).astype(BF16)
            GW1[:, pl.ds(mine, HALF)] = total[:, :HALF]
            GW1[:, pl.ds(theirs, HALF)] = total[:, HALF:]
        else:
            total = dot(H[0], X[1], (0, 0)).astype(BF16)
            GW2[pl.ds(mine, HALF), :] = total[:HALF]
            GW2[pl.ds(theirs, HALF), :] = total[HALF:]

    def e1():
        for s in (1, 2, 3, 4):
            for d in ways(s):
                ra_copy(s, d).wait_recv()
        total = G[pl.ds(0, 4 * ROWS), pl.ds(0, ZA)].astype(F32)
        for i in range(7):
            total += RA[i].astype(F32)
        OUT[:, pl.ds(0, ZA)] = total[:ROWS]
        SA[...] = total.astype(BF16)
        for f in (3, 1, 2):
            start(rx_copy(f))

    def e2():
        for s in (1, 2, 3, 4):
            for d in ways(s):
                rz_copy(s, d).wait_recv()
        total = OUT[:, pl.ds(ZA, ZB)]
        for i in range(7):
            total += RZ[i].astype(F32)
        GIN[:, pl.ds(ZA, ZB)] = total.astype(BF16)

    def e3():
        for f in (1, 2, 3):
            rx_copy(f).wait_recv()
        total = OUT[:, pl.ds(0, ZA)]
        for i in range(3):
            total += RX[i].astype(F32)
        GIN[:, pl.ds(0, ZA)] = total.astype(BF16)

    def drain():
        for copy in unsent:
            copy.wait_send()
        unsent.clear()

    steps = {
        "init": begin, "ax": ax, "az": az, "bz": bz, "bx": bx, "S1": s1, "S2": s2, "S3": s3, "S4": s4, "S5": s5, "S6": s6,
        "W": w, "E1": e1, "E2": e2, "E3": e3, "drain": drain,
    }
    for name, *args in ORDER:
        steps[name](*args)
    drain()


def write_out(a, b, c, a_hbm, b_hbm, c_hbm, sem):
    copies = [pltpu.make_async_copy(a, a_hbm, sem.at[0])]
    for i, (src, dst) in enumerate(((b, b_hbm), (c, c_hbm))):
        n = src.shape[0] // 2
        for j in range(2):
            part = pl.ds(j * n, n)
            copies.append(pltpu.make_async_copy(src.at[part], dst.at[part], sem.at[1 + 2 * i + j]))
    for copy in copies:
        copy.start()
    for copy in copies:
        copy.wait()


def per_device(tokens, grad_out, w_in, w_out):
    hbm, vmem = pl.BlockSpec(memory_space=pltpu.HBM), pl.BlockSpec(memory_space=pltpu.VMEM)
    dma = pltpu.SemaphoreType.DMA
    scratch = [
        pltpu.VMEM((2, TOK, D), BF16),
        pltpu.VMEM((D, FF), BF16),
        pltpu.VMEM((FF, D), BF16),
        pltpu.VMEM((2, TOK, HALF), BF16),
        pltpu.VMEM((2, TOK, HALF), F32),
        pltpu.VMEM((2, TOK, HALF), BF16),
        pltpu.VMEM((2, TOK, HALF), BF16),
        pltpu.VMEM((3, 2, TOK // 4, HALF), BF16),
        pltpu.VMEM((2, TOK, FF), BF16),
        pltpu.VMEM((TOK, D), BF16),
        pltpu.VMEM((7, 4 * ROWS, ZA), BF16),
        pltpu.VMEM((4 * ROWS, ZA), BF16),
        pltpu.VMEM((3, ROWS, ZA), BF16),
        pltpu.VMEM((9, 3, ROWS, ZB), BF16),
        pltpu.VMEM((7, ROWS, ZB), BF16),
        pltpu.VMEM((7, ROWS, ZB), BF16),
        pltpu.VMEM((ROWS, D), F32),
        dma((6,)),
    ]
    for shape in ((64,), (64,), (5,), (5, 3), (5, 3), (5,), (7,), (9, 3), (3,), (7,)):
        scratch += [dma(shape), dma(shape)]
    results = (
        jax.ShapeDtypeStruct((ROWS, D), BF16),
        jax.ShapeDtypeStruct((D, FF), BF16),
        jax.ShapeDtypeStruct((FF, D), BF16),
    )
    held = pl.pallas_call(
        kernel,
        out_shape=tuple(pltpu.VMEM(r.shape, r.dtype) for r in results),
        in_specs=[hbm] * 4,
        out_specs=(vmem, vmem, vmem),
        scratch_shapes=scratch,
        compiler_params=pltpu.CompilerParams(collective_id=0, has_side_effects=True, vmem_limit_bytes=40 * 2**20),
        cost_estimate=pl.CostEstimate(flops=10 * TOK * D * FF, bytes_accessed=8 * D * FF, transcendentals=TOK * HALF // 4),
    )(*(pltpu.with_memory_space_constraint(arg, pltpu.HBM) for arg in (tokens, grad_out, w_in, w_out)))
    return pl.pallas_call(
        write_out,
        out_shape=tuple(pltpu.HBM(r.shape, r.dtype) for r in results),
        in_specs=[vmem] * 3,
        out_specs=(hbm, hbm, hbm),
        scratch_shapes=[dma((5,))],
        cost_estimate=pl.CostEstimate(flops=0, bytes_accessed=8 * D * FF, transcendentals=0),
    )(*held)


def solution(mesh):
    return jax.shard_map(
        per_device,
        mesh=mesh,
        in_specs=(P("col", "row"), P("col", "row"), P("row", "col"), P("col", "row")),
        out_specs=(P("col", "row"), P("row", "col"), P("col", "row")),
        check_vma=False,
    )
```

```python
import math

import jax
import jax.numpy as jnp
from jax import lax
from jax.experimental import pallas as pl
from jax.experimental.pallas import tpu as pltpu
from jax.sharding import PartitionSpec as P

F32, BF16 = jnp.float32, jnp.bfloat16
MESH = pl.DeviceIdType.MESH
D, FF, TOK = 1536, 768, 512
HALF = FF // 2
ROWS = 16
DIRECT = (4,)
CA = 640
ZA = 384
ZB = D - ZA
GROUPS = ((0, 4), (4, 8), (12, 8), (20, 8), (28, 4))
XOFF = (0, 1, -1, 2)
ORDER = (
    ("z", 1, 0, 0, 0), ("x", 0, 0, 0), ("T", 2, 0), ("T", 2, 1), ("z", 0, 0, 0, 0), ("T", 2, 2), ("x", 1, 0, 0),
    ("f", 0, 0, 0, 1), ("f", 0, 0, 0, 2), ("z", 1, 1, 1, 0), ("x", 1, 1, 0), ("z", 1, 1, 0, 0), ("x", 1, 1, 1),
    ("z", 0, 0, 0, 2), ("T", 1, 1), ("z", 0, 0, 0, 3), ("f", 1, 0, 0, 2), ("z", 0, 0, 0, 1), ("f", 1, 0, 0, 1),
    ("x", 1, 2, 1), ("x", 1, 2, 0), ("z", 1, 2, 0, 0), ("z", 0, 1, 1, 0), ("z", 0, 1, 0, 0), ("f", 1, 1, 1, 1),
    ("z", 1, 2, 1, 0), ("z", 0, 1, 0, 3), ("f", 1, 1, 0, 1), ("f", 1, 1, 0, 2), ("T", 1, 0), ("z", 0, 1, 1, 2),
    ("f", 1, 1, 1, 2), ("P", 0), ("z", 0, 1, 0, 1), ("f", 1, 2, 1, 1), ("f", 1, 2, 1, 2), ("Q", 0), ("x", 1, 3, 0),
    ("z", 0, 1, 0, 2), ("z", 0, 1, 1, 1), ("z", 1, 3, 0, 0), ("f", 1, 2, 0, 1), ("f", 1, 2, 0, 2), ("x", 1, 3, 1),
    ("z", 1, 3, 1, 0), ("z", 0, 1, 1, 3), ("z", 0, 2, 1, 0), ("z", 0, 2, 0, 0), ("T", 1, 5), ("S2", 0),
    ("z", 0, 2, 0, 3), ("P", 1), ("Q", 1), ("f", 1, 3, 0, 1), ("f", 1, 3, 0, 2), ("z", 0, 2, 1, 2), ("z", 0, 2, 0, 1),
    ("z", 0, 2, 0, 2), ("S2", 1), ("z", 0, 2, 1, 1), ("P", 2), ("z", 0, 2, 1, 3), ("f", 1, 3, 1, 2), ("f", 1, 3, 1, 1),
    ("Q", 2), ("z", 0, 3, 1, 0), ("S2", 2), ("z", 0, 3, 0, 0), ("x", 1, 4, 0), ("P", 3), ("z", 0, 3, 1, 1),
    ("z", 0, 3, 0, 2), ("S3", 1), ("Q", 3), ("z", 0, 3, 0, 1), ("z", 0, 3, 1, 2), ("z", 0, 3, 1, 3), ("z", 0, 3, 0, 3),
    ("T", 1, 2), ("S2", 3), ("T", 1, 4), ("S3", 2), ("P", 4), ("Q", 4), ("S4", 1), ("S2", 4), ("T", 1, 3), ("S3", 3),
    ("S5", 1), ("S3", 0), ("S4", 2), ("S3", 4), ("S5", 2), ("S4", 3), ("S6", 1, 1), ("S4", 0), ("S6", 1, 0), ("S5", 3),
    ("S4", 4), ("S5", 4), ("S5", 0), ("S6", 2, 1), ("S6", 2, 0), ("S6", 4, 0), ("S6", 3, 0), ("S6", 3, 1), ("W", 0),
    ("E1",), ("S6", 0, 0), ("W", 1), ("E3",), ("E2",),
)


def ways(s):
    return (0, 1) if s in (1, 2, 3) else (0,)


def block(s, d, f):
    return GROUPS[s][0] + 4 * d + f


def gelu_pair(pre_act, back_act):
    coeff = math.sqrt(2.0 / math.pi)
    inner = coeff * (pre_act + 0.044715 * pre_act * pre_act * pre_act)
    tanh_val = jnp.tanh(inner)
    activated = (0.5 * pre_act * (1.0 + tanh_val)).astype(BF16)
    slope = 0.5 * (1.0 + tanh_val) + 0.5 * pre_act * (1.0 - tanh_val * tanh_val) * coeff * (
        1.0 + 3.0 * 0.044715 * pre_act * pre_act
    )
    return activated, (back_act * slope).astype(BF16)


def dot(a, b, dims):
    return lax.dot_general(a, b, ((dims[:1], dims[1:]), ((), ())), preferred_element_type=F32)


def kernel(
    tok_hbm, grad_hbm, win_hbm, wout_hbm, GIN, GW1, GW2,
    X, W1, W2, W1T, W2T, KS, KO, KR, C, R, H, G, RA, SA, RX, RB, SB, RZ, OUT,
    local_sem, sent,
    a_recv, b_recv, k_recv, r_recv, y_recv, h_recv, ra_recv, rb_recv, rx_recv, rz_recv,
):
    row, col = lax.axis_index("row"), lax.axis_index("col")
    y, core, z, x = row // 2, row % 2, col // 4, col % 4

    def at(dz=0, dx=0, dy=0, other=False):
        return {
            "row": lax.rem(y + dy + 4, 4) * 2 + (1 - core if other else core),
            "col": lax.rem(z + dz + 8, 8) * 4 + lax.rem(x + dx + 4, 4),
        }

    mine = pl.multiple_of(core * HALF, HALF)
    theirs = pl.multiple_of((1 - core) * HALF, HALF)
    local = [
        pltpu.make_async_copy(tok_hbm, X.at[0, pl.ds(0, ROWS)], local_sem.at[0]),
        pltpu.make_async_copy(grad_hbm, X.at[1, pl.ds(0, ROWS)], local_sem.at[1]),
        pltpu.make_async_copy(win_hbm.at[:, pl.ds(mine, HALF)], W1.at[:, pl.ds(0, HALF)], local_sem.at[2]),
        pltpu.make_async_copy(win_hbm.at[:, pl.ds(theirs, HALF)], W1.at[:, pl.ds(HALF, HALF)], local_sem.at[3]),
        pltpu.make_async_copy(wout_hbm.at[pl.ds(mine, HALF)], W2.at[pl.ds(0, HALF)], local_sem.at[4]),
        pltpu.make_async_copy(wout_hbm.at[pl.ds(theirs, HALF)], W2.at[pl.ds(HALF, HALF)], local_sem.at[5]),
    ]
    for copy in local:
        copy.start()

    partners = [at(dz=i) for i in range(1, 8)] + [at(dx=i) for i in range(1, 4)] + [at(dy=i) for i in range(1, 4)]
    partners.append(at(other=True))
    barrier = pltpu.get_barrier_semaphore()
    for partner in partners:
        pl.semaphore_signal(barrier, inc=1, device_id=partner, device_id_type=MESH)
    pl.semaphore_wait(barrier, len(partners))

    done = set()

    def once(key):
        new = key not in done
        done.add(key)
        return new

    def remote(src, dst, kind, recv, target):
        return pltpu.make_async_remote_copy(
            src_ref=src, dst_ref=dst, send_sem=sent.at[kind], recv_sem=recv, device_id=target, device_id_type=MESH
        )

    def piece(part, s, d, f, which):
        array = pl.ds(0, 2) if which is None else pl.ds(which, 1)
        columns = pl.ds(0, CA) if part == 0 else pl.ds(CA, D - CA)
        return X.at[array, pl.ds(ROWS * block(s, d, f), ROWS), columns]

    def gather(part, src, dst, target, which=None):
        recv = (a_recv, b_recv)[part].at[block(*dst)]
        return remote(piece(part, *src, which), piece(part, *dst, which), part, recv, target)

    def arrived(part, s, d, f):
        if s == f == 0:
            if once("own"):
                local[0].wait()
                local[1].wait()
        elif once((part, s, d, f)):
            gather(part, (s, d, f), (s, d, f), at(dz=1)).wait_recv()

    def along_z(part, s, d, f):
        arrived(part, s, d, f)
        if s == 0:
            gather(part, (0, 0, f), (1, 0, f), at(dz=1)).start()
            gather(part, (0, 0, f), (1, 1, f), at(dz=-1)).start()
        elif s < 3:
            gather(part, (s, d, f), (s + 1, d, f), at(dz=-1 if d else 1)).start()
        else:
            gather(part, (3, d, f), (4, 0, f), at(dz=-1 if d else 1), d).start()

    def along_x(part, s, d):
        arrived(part, s, d, 0)
        gather(part, (s, d, 0), (s, d, 2), at(dx=1)).start()
        gather(part, (s, d, 0), (s, d, 1), at(dx=-1)).start()
        if part == 1 and s in DIRECT:
            gather(part, (s, d, 0), (s, d, 3), at(dx=2)).start()

    def further_x(part, s, d, f):
        arrived(part, s, d, f)
        gather(part, (s, d, f), (s, d, 3), at(dx=-1 if f == 1 else 1), f - 1).start()

    def weights(i):
        if once(("weights", i)):
            local[2 * i].wait()
            local[2 * i + 1].wait()

    def turn(i, j):
        weights(i)
        part = pl.ds(256 * j, 256)
        if i == 1:
            W1T[:, part] = W1[part, :].T
        else:
            W2T[:, part] = W2[part, :].T

    def rows(s):
        return ROWS * GROUPS[s][0], ROWS * GROUPS[s][1]

    def swap_copy(s, i):
        first, n = rows(s)
        part = pl.ds(first, n)
        return remote(KS.at[i, part], KR.at[i, part], 2, k_recv.at[s, i], at(other=True))

    def product(s, i):
        first, n = rows(s)
        part = pl.ds(first, n)
        total = dot(X[i, part, :], (W1, W2T)[i][...], (1, 0))
        KO[i, part, :] = total[:, :HALF]
        KS[i, part, :] = total[:, HALF:].astype(BF16)
        swap_copy(s, i).start()

    def p(s):
        for d in ways(s):
            for f in range(4):
                arrived(0, s, d, f)
                arrived(1, s, d, f)
        weights(1)
        product(s, 0)

    def q(s):
        product(s, 1)

    def quarter(s, i):
        first, n = rows(s)
        return pl.ds(pl.multiple_of(first + i * (n // 4), ROWS), n // 4)

    def sum_copy(s, dy):
        n = rows(s)[1] // 4
        there = R.at[dy - 1, :, pl.ds(rows(s)[0] // 4, n)]
        return remote(C.at[:, quarter(s, lax.rem(y + dy, 4))], there, 3, r_recv.at[s], at(dy=dy))

    def s2(s):
        first, n = rows(s)
        part = pl.ds(first, n)
        swap_copy(s, 0).wait_recv()
        swap_copy(s, 1).wait_recv()
        C[:, part, :] = (KO[:, part, :] + KR[:, part, :].astype(F32)).astype(BF16)
        for dy in (2, 1, 3):
            sum_copy(s, dy).start()

    def part_copy(s, dy):
        where = H.at[:, quarter(s, y), pl.ds(0, HALF)]
        return remote(where, where, 4, y_recv.at[s], at(dy=dy))

    def s3(s):
        part = pl.ds(rows(s)[0] // 4, rows(s)[1] // 4)
        landed = R.at[:, :, part]
        remote(landed, landed, 3, r_recv.at[s], at(dy=1)).wait_recv()
        total = C[:, quarter(s, y), :].astype(F32)
        for i in range(3):
            total += R[i, :, part, :].astype(F32)
        activated, grad_pre = gelu_pair(total[0], total[1])
        H[0, quarter(s, y), 0:HALF] = activated
        H[1, quarter(s, y), 0:HALF] = grad_pre
        for dy in (2, 1, 3):
            part_copy(s, dy).start()

    def half_copy(s):
        first, n = rows(s)
        part = pl.ds(first, n)
        return remote(H.at[:, part, pl.ds(0, HALF)], H.at[:, part, pl.ds(HALF, HALF)], 5, h_recv.at[s], at(other=True))

    def s4(s):
        first, n = rows(s)
        landed = H.at[:, pl.ds(first, 3 * n // 4), pl.ds(0, HALF)]
        remote(landed, landed, 4, y_recv.at[s], at(dy=1)).wait_recv()
        half_copy(s).start()

    def ra_copy(s, d):
        i = 2 * (s - 1) + d
        src = G.at[pl.ds(ROWS * block(s, d, 0), 4 * ROWS), pl.ds(0, ZA)]
        return remote(src, RA.at[i], 6, ra_recv, at(dz=s if d else -s))

    def rb_copy(s, d, f):
        i = 2 * s + d
        src = G.at[pl.ds(ROWS * block(s, d, f), ROWS), pl.ds(ZA, ZB)]
        return remote(src, RB.at[i, f - 1], 7, rb_recv.at[i], at(dx=XOFF[f]))

    def rz_copy(s, d):
        i = 2 * (s - 1) + d
        return remote(SB.at[i], RZ.at[i], 8, rz_recv, at(dz=s if d else -s))

    def rx_copy(f):
        src = SA.at[pl.ds(ROWS * f, ROWS)]
        return remote(src, RX.at[f - 1], 9, rx_recv, at(dx=XOFF[f]))

    def s5(s):
        half_copy(s).wait_recv()
        first, n = rows(s)
        part = pl.ds(first, n)
        G[part, :] = dot(H[1, part, :], W1T[...], (1, 0)).astype(BF16)
        for d in ways(s):
            for f in (3, 1, 2):
                rb_copy(s, d, f).start()
            if s:
                ra_copy(s, d).start()

    def s6(s, d):
        i = 2 * s + d
        remote(RB.at[i], RB.at[i], 7, rb_recv.at[i], at(dx=1)).wait_recv()
        total = G[pl.ds(ROWS * block(s, d, 0), ROWS), pl.ds(ZA, ZB)].astype(F32)
        for j in range(3):
            total += RB[i, j].astype(F32)
        if s:
            SB[2 * (s - 1) + d] = total.astype(BF16)
            rz_copy(s, d).start()
        else:
            OUT[:, pl.ds(ZA, ZB)] = total

    def w(i):
        if i == 0:
            total = dot(X[0], H[1], (0, 0)).astype(BF16)
            GW1[:, pl.ds(mine, HALF)] = total[:, :HALF]
            GW1[:, pl.ds(theirs, HALF)] = total[:, HALF:]
        else:
            total = dot(H[0], X[1], (0, 0)).astype(BF16)
            GW2[pl.ds(mine, HALF), :] = total[:HALF]
            GW2[pl.ds(theirs, HALF), :] = total[HALF:]

    def e1():
        remote(RA, RA, 6, ra_recv, at(dz=1)).wait_recv()
        total = G[pl.ds(0, 4 * ROWS), pl.ds(0, ZA)].astype(F32)
        for i in range(7):
            total += RA[i].astype(F32)
        OUT[:, pl.ds(0, ZA)] = total[:ROWS]
        SA[...] = total.astype(BF16)
        for f in (3, 1, 2):
            rx_copy(f).start()

    def e2():
        remote(RZ, RZ, 8, rz_recv, at(dz=1)).wait_recv()
        total = OUT[:, pl.ds(ZA, ZB)]
        for i in range(7):
            total += RZ[i].astype(F32)
        GIN[:, pl.ds(ZA, ZB)] = total.astype(BF16)

    def e3():
        remote(RX, RX, 9, rx_recv, at(dx=1)).wait_recv()
        total = OUT[:, pl.ds(0, ZA)]
        for i in range(3):
            total += RX[i].astype(F32)
        GIN[:, pl.ds(0, ZA)] = total.astype(BF16)

    steps = {
        "z": along_z, "x": along_x, "f": further_x, "T": turn, "P": p, "Q": q, "S2": s2, "S3": s3, "S4": s4, "S5": s5,
        "S6": s6, "W": w, "E1": e1, "E2": e2, "E3": e3,
    }
    for name, *args in ORDER:
        steps[name](*args)
    moved = 31 * ROWS
    for kind, ref in enumerate((
        X.at[:, pl.ds(0, moved), pl.ds(0, CA)],
        X.at[:, pl.ds(0, moved), pl.ds(CA, D - CA)],
        KS,
        C.at[:, pl.ds(0, 3 * TOK // 4)],
        H.at[:, pl.ds(0, 3 * TOK // 4), pl.ds(0, HALF)],
        H.at[:, :, pl.ds(0, HALF)],
        RA,
        G.at[pl.ds(0, 24 * ROWS), pl.ds(ZA, ZB)],
        SB,
        RX,
    )):
        remote(ref, ref, kind, rx_recv, at(dz=1)).wait_send()


def write_out(a, b, c, a_hbm, b_hbm, c_hbm, sem):
    copies = [pltpu.make_async_copy(a, a_hbm, sem.at[0])]
    for i, (src, dst) in enumerate(((b, b_hbm), (c, c_hbm))):
        n = src.shape[0] // 2
        for j in range(2):
            part = pl.ds(j * n, n)
            copies.append(pltpu.make_async_copy(src.at[part], dst.at[part], sem.at[1 + 2 * i + j]))
    for copy in copies:
        copy.start()
    for copy in copies:
        copy.wait()


def per_device(tokens, grad_out, w_in, w_out):
    hbm, vmem = pl.BlockSpec(memory_space=pltpu.HBM), pl.BlockSpec(memory_space=pltpu.VMEM)
    dma = pltpu.SemaphoreType.DMA
    scratch = [
        pltpu.VMEM((2, TOK, D), BF16),
        pltpu.VMEM((D, FF), BF16),
        pltpu.VMEM((FF, D), BF16),
        pltpu.VMEM((FF, D), BF16),
        pltpu.VMEM((D, FF), BF16),
        pltpu.VMEM((2, TOK, HALF), BF16),
        pltpu.VMEM((2, TOK, HALF), F32),
        pltpu.VMEM((2, TOK, HALF), BF16),
        pltpu.VMEM((2, TOK, HALF), BF16),
        pltpu.VMEM((3, 2, TOK // 4, HALF), BF16),
        pltpu.VMEM((2, TOK, FF), BF16),
        pltpu.VMEM((TOK, D), BF16),
        pltpu.VMEM((7, 4 * ROWS, ZA), BF16),
        pltpu.VMEM((4 * ROWS, ZA), BF16),
        pltpu.VMEM((3, ROWS, ZA), BF16),
        pltpu.VMEM((9, 3, ROWS, ZB), BF16),
        pltpu.VMEM((7, ROWS, ZB), BF16),
        pltpu.VMEM((7, ROWS, ZB), BF16),
        pltpu.VMEM((ROWS, D), F32),
        dma((6,)),
        dma((10,)),
    ]
    for shape in ((32,), (32,), (5, 2), (5,), (5,), (5,), (), (9,), (), ()):
        scratch.append(dma(shape))
    results = (
        jax.ShapeDtypeStruct((ROWS, D), BF16),
        jax.ShapeDtypeStruct((D, FF), BF16),
        jax.ShapeDtypeStruct((FF, D), BF16),
    )
    held = pl.pallas_call(
        kernel,
        out_shape=tuple(pltpu.VMEM(r.shape, r.dtype) for r in results),
        in_specs=[hbm] * 4,
        out_specs=(vmem, vmem, vmem),
        scratch_shapes=scratch,
        compiler_params=pltpu.CompilerParams(collective_id=0, has_side_effects=True, vmem_limit_bytes=40 * 2**20),
        cost_estimate=pl.CostEstimate(flops=10 * TOK * D * FF, bytes_accessed=8 * D * FF, transcendentals=TOK * HALF // 4),
    )(*(pltpu.with_memory_space_constraint(arg, pltpu.HBM) for arg in (tokens, grad_out, w_in, w_out)))
    return pl.pallas_call(
        write_out,
        out_shape=tuple(pltpu.HBM(r.shape, r.dtype) for r in results),
        in_specs=[vmem] * 3,
        out_specs=(hbm, hbm, hbm),
        scratch_shapes=[dma((5,))],
        compiler_params=pltpu.CompilerParams(vmem_limit_bytes=8 * 2**20),
        cost_estimate=pl.CostEstimate(flops=0, bytes_accessed=8 * D * FF, transcendentals=0),
    )(*(pltpu.with_memory_space_constraint(array, pltpu.VMEM) for array in held))


def solution(mesh):
    return jax.shard_map(
        per_device,
        mesh=mesh,
        in_specs=(P("col", "row"), P("col", "row"), P("row", "col"), P("col", "row")),
        out_specs=(P("col", "row"), P("row", "col"), P("col", "row")),
        check_vma=False,
    )
```

```python
import math

import jax
import jax.numpy as jnp
from jax import lax
from jax.experimental import pallas as pl
from jax.experimental.pallas import tpu as pltpu
from jax.sharding import PartitionSpec as P

F32, BF16 = jnp.float32, jnp.bfloat16
MESH = pl.DeviceIdType.MESH
D, FF, TOK = 1536, 768, 512
HALF = FF // 2
ROWS = 16
DIRECT = (4,)
CA = 640
ZA = 256
ZB = D - ZA
GROUPS = ((0, 4), (4, 8), (12, 8), (20, 8), (28, 4))
MERGE = True
ZSLOT = {1: 0, 2: 2, 4: 4} if MERGE else {1: 0, 2: 2, 3: 4, 4: 6}
ZSUMS = 5 if MERGE else 7
XOFF = (0, 1, -1, 2)
ORDER = (
    ("z", 1, 0, 0, 0), ("x", 0, 0, 0), ("z", 0, 0, 0, 0), ("x", 1, 0, 0), ("f", 0, 0, 0, 1), ("f", 0, 0, 0, 2),
    ("z", 1, 1, 0, 0), ("z", 1, 1, 1, 0), ("x", 1, 1, 1), ("T", 1, 4), ("x", 1, 1, 0), ("f", 1, 0, 0, 2),
    ("z", 0, 0, 0, 1), ("T", 1, 2), ("z", 0, 0, 0, 2), ("T", 2, 2), ("f", 1, 0, 0, 1), ("z", 0, 0, 0, 3),
    ("x", 1, 2, 0), ("T", 1, 1), ("f", 1, 1, 1, 2), ("z", 1, 2, 0, 0), ("z", 0, 1, 0, 0), ("z", 1, 2, 1, 0),
    ("f", 1, 1, 1, 1), ("z", 0, 1, 1, 0), ("T", 2, 1), ("f", 1, 1, 0, 2), ("f", 1, 1, 0, 1), ("z", 0, 1, 1, 2),
    ("x", 1, 2, 1), ("T", 2, 0), ("z", 0, 1, 0, 1), ("z", 0, 1, 0, 3), ("T", 1, 3), ("z", 0, 1, 0, 2),
    ("z", 0, 1, 1, 3), ("f", 1, 2, 0, 1), ("f", 1, 2, 0, 2), ("x", 1, 3, 1), ("z", 1, 3, 1, 0), ("z", 0, 1, 1, 1),
    ("z", 1, 3, 0, 0), ("P", 1), ("Q", 1), ("x", 1, 3, 0), ("f", 1, 2, 1, 1), ("z", 0, 2, 1, 0), ("z", 0, 2, 1, 2),
    ("f", 1, 2, 1, 2), ("z", 0, 2, 0, 0), ("P", 0), ("z", 0, 2, 0, 1), ("z", 0, 2, 1, 3), ("S2", 1), ("z", 0, 2, 0, 3),
    ("T", 1, 5), ("z", 0, 2, 0, 2), ("f", 1, 3, 1, 1), ("Q", 0), ("z", 0, 2, 1, 1), ("f", 1, 3, 1, 2),
    ("f", 1, 3, 0, 2), ("f", 1, 3, 0, 1), ("x", 1, 4, 0), ("S2", 0), ("P", 2), ("Q", 2), ("S3", 1, 0),
    ("z", 0, 3, 0, 3), ("z", 0, 3, 1, 0), ("z", 0, 3, 0, 0), ("T", 1, 0), ("z", 0, 3, 1, 2), ("z", 0, 3, 0, 1),
    ("z", 0, 3, 1, 3), ("S3", 1, 1), ("z", 0, 3, 0, 2), ("P", 3), ("Q", 3), ("S2", 2), ("z", 0, 3, 1, 1), ("S2", 3),
    ("P", 4), ("Q", 4), ("S4", 1, 0), ("S4", 1, 1), ("S3", 2, 0), ("S2", 4), ("S5", 1, 1), ("S3", 3, 0), ("S5", 1, 0),
    ("S3", 3, 1), ("S3", 2, 1), ("S4", 2, 0), ("S3", 4, 0), ("S5", 2, 0), ("S4", 3, 0), ("S3", 0, 0), ("S4", 3, 1),
    ("S5", 3, 0), ("S6", 1, 0), ("S5", 3, 1), ("S4", 4, 0), ("S4", 2, 1), ("S6", 1, 1), ("S4", 0, 0), ("S5", 4, 0),
    ("S5", 2, 1), ("S6", 2, 0), ("S5", 0, 0), ("MA", 1), ("S6", 3, 0), ("MA", 0), ("S6", 3, 1), ("W", 1, 1),
    ("W", 1, 0), ("S6", 4, 0), ("MZ", 0), ("S6", 2, 1), ("MZ", 1), ("E1",), ("W", 0, 0), ("S6", 0, 0), ("W", 0, 1),
    ("E3",), ("E2",),
)


def ways(s):
    return (0, 1) if s in (1, 2, 3) else (0,)


def block(s, d, f):
    return GROUPS[s][0] + 4 * d + f


def gelu_pair(pre_act, back_act):
    coeff = math.sqrt(2.0 / math.pi)
    inner = coeff * (pre_act + 0.044715 * pre_act * pre_act * pre_act)
    tanh_val = jnp.tanh(inner)
    activated = (0.5 * pre_act * (1.0 + tanh_val)).astype(BF16)
    slope = 0.5 * (1.0 + tanh_val) + 0.5 * pre_act * (1.0 - tanh_val * tanh_val) * coeff * (
        1.0 + 3.0 * 0.044715 * pre_act * pre_act
    )
    return activated, (back_act * slope).astype(BF16)


def dot(a, b, dims):
    return lax.dot_general(a, b, ((dims[:1], dims[1:]), ((), ())), preferred_element_type=F32)


def kernel(
    tok_hbm, grad_hbm, win_hbm, wout_hbm, GIN, GW1, GW2,
    X, W1, W2, W1T, W2T, KS, KO, KR, C, R, H, G, RA, RM, SA, RX, RB, SB, HOLD, RZ, RN, OUT,
    local_sem, sent,
    a_recv, b_recv, k_recv, r_recv, y_recv, h_recv, ra_recv, rb_recv, rx_recv, rz_recv,
):
    row, col = lax.axis_index("row"), lax.axis_index("col")
    y, core, z, x = row // 2, row % 2, col // 4, col % 4

    def at(dz=0, dx=0, dy=0, other=False):
        return {
            "row": lax.rem(y + dy + 4, 4) * 2 + (1 - core if other else core),
            "col": lax.rem(z + dz + 8, 8) * 4 + lax.rem(x + dx + 4, 4),
        }

    mine = pl.multiple_of(core * HALF, HALF)
    theirs = pl.multiple_of((1 - core) * HALF, HALF)
    local = [
        pltpu.make_async_copy(tok_hbm, X.at[0, pl.ds(0, ROWS)], local_sem.at[0]),
        pltpu.make_async_copy(grad_hbm, X.at[1, pl.ds(0, ROWS)], local_sem.at[1]),
        pltpu.make_async_copy(win_hbm.at[:, pl.ds(mine, HALF)], W1.at[:, pl.ds(0, HALF)], local_sem.at[2]),
        pltpu.make_async_copy(win_hbm.at[:, pl.ds(theirs, HALF)], W1.at[:, pl.ds(HALF, HALF)], local_sem.at[3]),
        pltpu.make_async_copy(wout_hbm.at[pl.ds(mine, HALF)], W2.at[pl.ds(0, HALF)], local_sem.at[4]),
        pltpu.make_async_copy(wout_hbm.at[pl.ds(theirs, HALF)], W2.at[pl.ds(HALF, HALF)], local_sem.at[5]),
    ]
    for copy in local:
        copy.start()

    partners = [at(dz=i) for i in range(1, 8)] + [at(dx=i) for i in range(1, 4)] + [at(dy=i) for i in range(1, 4)]
    partners.append(at(other=True))
    barrier = pltpu.get_barrier_semaphore()
    for partner in partners:
        pl.semaphore_signal(barrier, inc=1, device_id=partner, device_id_type=MESH)
    pl.semaphore_wait(barrier, len(partners))

    done = set()

    def once(key):
        new = key not in done
        done.add(key)
        return new

    def remote(src, dst, kind, recv, target):
        return pltpu.make_async_remote_copy(
            src_ref=src, dst_ref=dst, send_sem=sent.at[kind], recv_sem=recv, device_id=target, device_id_type=MESH
        )

    def piece(part, s, d, f, which):
        array = pl.ds(0, 2) if which is None else pl.ds(which, 1)
        columns = pl.ds(0, CA) if part == 0 else pl.ds(CA, D - CA)
        return X.at[array, pl.ds(ROWS * block(s, d, f), ROWS), columns]

    def gather(part, src, dst, target, which=None):
        recv = (a_recv, b_recv)[part].at[block(*dst)]
        return remote(piece(part, *src, which), piece(part, *dst, which), part, recv, target)

    def arrived(part, s, d, f):
        if s == f == 0:
            if once("own"):
                local[0].wait()
                local[1].wait()
        elif once((part, s, d, f)):
            gather(part, (s, d, f), (s, d, f), at(dz=1)).wait_recv()

    def along_z(part, s, d, f):
        arrived(part, s, d, f)
        if s == 0:
            gather(part, (0, 0, f), (1, 0, f), at(dz=1)).start()
            gather(part, (0, 0, f), (1, 1, f), at(dz=-1)).start()
        elif s < 3:
            gather(part, (s, d, f), (s + 1, d, f), at(dz=-1 if d else 1)).start()
        else:
            gather(part, (3, d, f), (4, 0, f), at(dz=-1 if d else 1), d).start()

    def along_x(part, s, d):
        arrived(part, s, d, 0)
        gather(part, (s, d, 0), (s, d, 2), at(dx=1)).start()
        gather(part, (s, d, 0), (s, d, 1), at(dx=-1)).start()
        if part == 1 and s in DIRECT:
            gather(part, (s, d, 0), (s, d, 3), at(dx=2)).start()

    def further_x(part, s, d, f):
        arrived(part, s, d, f)
        gather(part, (s, d, f), (s, d, 3), at(dx=-1 if f == 1 else 1), f - 1).start()

    def weights(i):
        if once(("weights", i)):
            local[2 * i].wait()
            local[2 * i + 1].wait()

    def turn(i, j):
        weights(i)
        part = pl.ds(256 * j, 256)
        if i == 1:
            W1T[:, part] = W1[part, :].T
        else:
            W2T[:, part] = W2[part, :].T

    def rows(s):
        return ROWS * GROUPS[s][0], ROWS * GROUPS[s][1]

    def swap_copy(s, i):
        first, n = rows(s)
        part = pl.ds(first, n)
        return remote(KS.at[i, part], KR.at[i, part], 2, k_recv.at[s, i], at(other=True))

    def product(s, i):
        first, n = rows(s)
        part = pl.ds(first, n)
        total = dot(X[i, part, :], (W1, W2T)[i][...], (1, 0))
        KO[i, part, :] = total[:, :HALF]
        KS[i, part, :] = total[:, HALF:].astype(BF16)
        swap_copy(s, i).start()

    def p(s):
        for d in ways(s):
            for f in range(4):
                arrived(0, s, d, f)
                arrived(1, s, d, f)
        weights(1)
        product(s, 0)

    def q(s):
        product(s, 1)

    def first(s, d):
        return ROWS * block(s, d, 0)

    def quarter(s, d, i):
        return pl.ds(pl.multiple_of(first(s, d) + i * ROWS, ROWS), ROWS)

    def sum_copy(s, d, dy):
        there = R.at[dy - 1, :, pl.ds(first(s, d) // 4, ROWS)]
        return remote(C.at[:, quarter(s, d, lax.rem(y + dy, 4))], there, 3, r_recv.at[2 * s + d], at(dy=dy))

    def s2(s):
        part = pl.ds(*rows(s))
        swap_copy(s, 0).wait_recv()
        swap_copy(s, 1).wait_recv()
        C[:, part, :] = (KO[:, part, :] + KR[:, part, :].astype(F32)).astype(BF16)
        for d in ways(s):
            for dy in (2, 1, 3):
                sum_copy(s, d, dy).start()

    def part_copy(s, d, dy):
        where = H.at[:, quarter(s, d, y), pl.ds(0, HALF)]
        return remote(where, where, 4, y_recv.at[2 * s + d], at(dy=dy))

    def s3(s, d):
        part = pl.ds(first(s, d) // 4, ROWS)
        landed = R.at[:, :, part]
        remote(landed, landed, 3, r_recv.at[2 * s + d], at(dy=1)).wait_recv()
        total = C[:, quarter(s, d, y), :].astype(F32)
        for i in range(3):
            total += R[i, :, part, :].astype(F32)
        activated, grad_pre = gelu_pair(total[0], total[1])
        H[0, quarter(s, d, y), 0:HALF] = activated
        H[1, quarter(s, d, y), 0:HALF] = grad_pre
        for dy in (2, 1, 3):
            part_copy(s, d, dy).start()

    def half_copy(s, d):
        part = pl.ds(first(s, d), 4 * ROWS)
        there = H.at[:, part, pl.ds(HALF, HALF)]
        return remote(H.at[:, part, pl.ds(0, HALF)], there, 5, h_recv.at[2 * s + d], at(other=True))

    def s4(s, d):
        landed = H.at[:, pl.ds(first(s, d), 3 * ROWS), pl.ds(0, HALF)]
        remote(landed, landed, 4, y_recv.at[2 * s + d], at(dy=1)).wait_recv()
        half_copy(s, d).start()

    def z_copy(src, s, d, kind, recv, straight, added):
        if MERGE and s == 3:
            return remote(src, added.at[d], kind, recv.at[1 + d], at(dz=1 if d else -1))
        return remote(src, straight.at[ZSLOT[s] + d], kind, recv.at[0], at(dz=s if d else -s))

    def ra_copy(s, d):
        return z_copy(G.at[pl.ds(first(s, d), 4 * ROWS), pl.ds(0, ZA)], s, d, 6, ra_recv, RA, RM)

    def rb_copy(s, d, f):
        i = 2 * s + d
        src = G.at[pl.ds(ROWS * block(s, d, f), ROWS), pl.ds(ZA, ZB)]
        return remote(src, RB.at[i, f - 1], 7, rb_recv.at[i], at(dx=XOFF[f]))

    def rz_copy(s, d):
        return z_copy(SB.at[2 * (s - 1) + d], s, d, 8, rz_recv, RZ, RN)

    def rx_copy(f):
        src = SA.at[pl.ds(ROWS * f, ROWS)]
        return remote(src, RX.at[f - 1], 9, rx_recv, at(dx=XOFF[f]))

    def s5(s, d):
        half_copy(s, d).wait_recv()
        part = pl.ds(first(s, d), 4 * ROWS)
        G[part, :] = dot(H[1, part, :], W1T[...], (1, 0)).astype(BF16)
        for f in (3, 1, 2):
            rb_copy(s, d, f).start()
        if s and not (MERGE and s == 2):
            ra_copy(s, d).start()

    def ma(d):
        remote(RM.at[d], RM.at[d], 6, ra_recv.at[1 + d], at(dz=1)).wait_recv()
        part = pl.ds(first(2, d), 4 * ROWS)
        G[part, pl.ds(0, ZA)] = (G[part, pl.ds(0, ZA)].astype(F32) + RM[d].astype(F32)).astype(BF16)
        ra_copy(2, d).start()

    def s6(s, d):
        i = 2 * s + d
        remote(RB.at[i], RB.at[i], 7, rb_recv.at[i], at(dx=1)).wait_recv()
        total = G[pl.ds(first(s, d), ROWS), pl.ds(ZA, ZB)].astype(F32)
        for j in range(3):
            total += RB[i, j].astype(F32)
        if s == 0:
            OUT[:, pl.ds(ZA, ZB)] = total
        elif MERGE and s == 2:
            HOLD[d] = total
        else:
            SB[2 * (s - 1) + d] = total.astype(BF16)
            rz_copy(s, d).start()

    def mz(d):
        remote(RN.at[d], RN.at[d], 8, rz_recv.at[1 + d], at(dz=1)).wait_recv()
        SB[2 + d] = (HOLD[d] + RN[d].astype(F32)).astype(BF16)
        rz_copy(2, d).start()

    def w(i, j):
        if i == 0:
            part = pl.ds(j * (D // 2), D // 2)
            total = dot(X[0, :, part], H[1], (0, 0)).astype(BF16)
            GW1[part, pl.ds(mine, HALF)] = total[:, :HALF]
            GW1[part, pl.ds(theirs, HALF)] = total[:, HALF:]
        else:
            total = dot(H[0, :, pl.ds(j * HALF, HALF)], X[1], (0, 0)).astype(BF16)
            GW2[pl.ds(theirs if j else mine, HALF), :] = total

    def e1():
        remote(RA, RA, 6, ra_recv.at[0], at(dz=1)).wait_recv()
        total = G[pl.ds(0, 4 * ROWS), pl.ds(0, ZA)].astype(F32)
        for i in range(ZSUMS):
            total += RA[i].astype(F32)
        OUT[:, pl.ds(0, ZA)] = total[:ROWS]
        SA[...] = total.astype(BF16)
        for f in (3, 1, 2):
            rx_copy(f).start()

    def e2():
        remote(RZ, RZ, 8, rz_recv.at[0], at(dz=1)).wait_recv()
        total = OUT[:, pl.ds(ZA, ZB)]
        for i in range(ZSUMS):
            total += RZ[i].astype(F32)
        GIN[:, pl.ds(ZA, ZB)] = total.astype(BF16)

    def e3():
        remote(RX, RX, 9, rx_recv, at(dx=1)).wait_recv()
        total = OUT[:, pl.ds(0, ZA)]
        for i in range(3):
            total += RX[i].astype(F32)
        GIN[:, pl.ds(0, ZA)] = total.astype(BF16)

    steps = {
        "z": along_z, "x": along_x, "f": further_x, "T": turn, "P": p, "Q": q, "S2": s2, "S3": s3, "S4": s4, "S5": s5,
        "S6": s6, "MA": ma, "MZ": mz, "W": w, "E1": e1, "E2": e2, "E3": e3,
    }
    for name, *args in ORDER:
        steps[name](*args)
    moved = 31 * ROWS
    for kind, ref in enumerate((
        X.at[:, pl.ds(0, moved), pl.ds(0, CA)],
        X.at[:, pl.ds(0, moved), pl.ds(CA, D - CA)],
        KS,
        C.at[:, pl.ds(0, 3 * TOK // 4)],
        H.at[:, pl.ds(0, 3 * TOK // 4), pl.ds(0, HALF)],
        H.at[:, :, pl.ds(0, HALF)],
        G.at[pl.ds(0, 28 * ROWS), pl.ds(0, ZA)],
        G.at[pl.ds(0, 24 * ROWS), pl.ds(ZA, ZB)],
        SB,
        RX,
    )):
        remote(ref, ref, kind, rx_recv, at(dz=1)).wait_send()


def write_out(a, b, c, a_hbm, b_hbm, c_hbm, sem):
    copies = [pltpu.make_async_copy(a, a_hbm, sem.at[0])]
    for i, (src, dst) in enumerate(((b, b_hbm), (c, c_hbm))):
        n = src.shape[0] // 2
        for j in range(2):
            part = pl.ds(j * n, n)
            copies.append(pltpu.make_async_copy(src.at[part], dst.at[part], sem.at[1 + 2 * i + j]))
    for copy in copies:
        copy.start()
    for copy in copies:
        copy.wait()


def per_device(tokens, grad_out, w_in, w_out):
    hbm, vmem = pl.BlockSpec(memory_space=pltpu.HBM), pl.BlockSpec(memory_space=pltpu.VMEM)
    dma = pltpu.SemaphoreType.DMA
    scratch = [
        pltpu.VMEM((2, TOK, D), BF16),
        pltpu.VMEM((D, FF), BF16),
        pltpu.VMEM((FF, D), BF16),
        pltpu.VMEM((FF, D), BF16),
        pltpu.VMEM((D, FF), BF16),
        pltpu.VMEM((2, TOK, HALF), BF16),
        pltpu.VMEM((2, TOK, HALF), F32),
        pltpu.VMEM((2, TOK, HALF), BF16),
        pltpu.VMEM((2, TOK, HALF), BF16),
        pltpu.VMEM((3, 2, TOK // 4, HALF), BF16),
        pltpu.VMEM((2, TOK, FF), BF16),
        pltpu.VMEM((TOK, D), BF16),
        pltpu.VMEM((ZSUMS, 4 * ROWS, ZA), BF16),
        pltpu.VMEM((2, 4 * ROWS, ZA), BF16),
        pltpu.VMEM((4 * ROWS, ZA), BF16),
        pltpu.VMEM((3, ROWS, ZA), BF16),
        pltpu.VMEM((9, 3, ROWS, ZB), BF16),
        pltpu.VMEM((7, ROWS, ZB), BF16),
        pltpu.VMEM((2, ROWS, ZB), F32),
        pltpu.VMEM((ZSUMS, ROWS, ZB), BF16),
        pltpu.VMEM((2, ROWS, ZB), BF16),
        pltpu.VMEM((ROWS, D), F32),
        dma((6,)),
        dma((10,)),
    ]
    for shape in ((32,), (32,), (5, 2), (9,), (9,), (9,), (3,), (9,), (), (3,)):
        scratch.append(dma(shape))
    results = (
        jax.ShapeDtypeStruct((ROWS, D), BF16),
        jax.ShapeDtypeStruct((D, FF), BF16),
        jax.ShapeDtypeStruct((FF, D), BF16),
    )
    held = pl.pallas_call(
        kernel,
        out_shape=tuple(pltpu.VMEM(r.shape, r.dtype) for r in results),
        in_specs=[hbm] * 4,
        out_specs=(vmem, vmem, vmem),
        scratch_shapes=scratch,
        compiler_params=pltpu.CompilerParams(collective_id=0, has_side_effects=True, vmem_limit_bytes=40 * 2**20),
        cost_estimate=pl.CostEstimate(flops=10 * TOK * D * FF, bytes_accessed=8 * D * FF, transcendentals=TOK * HALF // 4),
    )(*(pltpu.with_memory_space_constraint(arg, pltpu.HBM) for arg in (tokens, grad_out, w_in, w_out)))
    return pl.pallas_call(
        write_out,
        out_shape=tuple(pltpu.HBM(r.shape, r.dtype) for r in results),
        in_specs=[vmem] * 3,
        out_specs=(hbm, hbm, hbm),
        scratch_shapes=[dma((5,))],
        compiler_params=pltpu.CompilerParams(vmem_limit_bytes=8 * 2**20),
        cost_estimate=pl.CostEstimate(flops=0, bytes_accessed=8 * D * FF, transcendentals=0),
    )(*(pltpu.with_memory_space_constraint(array, pltpu.VMEM) for array in held))


def solution(mesh):
    return jax.shard_map(
        per_device,
        mesh=mesh,
        in_specs=(P("col", "row"), P("col", "row"), P("row", "col"), P("col", "row")),
        out_specs=(P("col", "row"), P("row", "col"), P("col", "row")),
        check_vma=False,
    )
```

```python
import math

import jax
import jax.numpy as jnp
from jax import lax
from jax.experimental import pallas as pl
from jax.experimental.pallas import tpu as pltpu
from jax.sharding import PartitionSpec as P

F32, BF16 = jnp.float32, jnp.bfloat16
MESH = pl.DeviceIdType.MESH
D, FF, TOK = 1536, 768, 512
HALF = FF // 2
ROWS = 16
DIRECT = (4,)
CA = 640
ZA = 256
ZB = D - ZA
GROUPS = ((0, 4), (4, 8), (12, 8), (20, 8), (28, 4))
MERGE = False
ZSLOT = {1: 0, 2: 2, 4: 4} if MERGE else {1: 0, 2: 2, 3: 4, 4: 6}
ZSUMS = 5 if MERGE else 7
XOFF = (0, 1, -1, 2)
ORDER = (
    ("z", 1, 0, 0, 0), ("x", 0, 0, 0), ("T", 1, 5), ("z", 0, 0, 0, 0), ("x", 1, 0, 0), ("T", 1, 1), ("z", 1, 1, 0, 0),
    ("f", 0, 0, 0, 2), ("f", 0, 0, 0, 1), ("z", 1, 1, 1, 0), ("x", 1, 1, 1), ("z", 0, 0, 0, 1), ("x", 1, 1, 0),
    ("T", 1, 2), ("T", 1, 0), ("T", 2, 1), ("f", 1, 0, 0, 2), ("T", 1, 3), ("z", 0, 0, 0, 2), ("f", 1, 0, 0, 1),
    ("z", 0, 1, 1, 0), ("z", 0, 1, 0, 0), ("x", 1, 2, 0), ("T", 1, 4), ("z", 0, 0, 0, 3), ("x", 1, 2, 1),
    ("z", 0, 1, 0, 1), ("f", 1, 1, 1, 1), ("z", 0, 1, 1, 1), ("f", 1, 1, 1, 2), ("z", 1, 2, 0, 0), ("T", 2, 0),
    ("f", 1, 1, 0, 1), ("z", 1, 2, 1, 0), ("f", 1, 1, 0, 2), ("z", 0, 1, 0, 2), ("T", 2, 2), ("z", 0, 1, 1, 2),
    ("P", 0), ("Q", 0), ("f", 1, 2, 0, 1), ("z", 0, 1, 0, 3), ("z", 0, 1, 1, 3), ("f", 1, 2, 0, 2), ("z", 0, 2, 1, 0),
    ("f", 1, 2, 1, 2), ("f", 1, 2, 1, 1), ("z", 0, 2, 0, 0), ("S2", 0), ("x", 1, 3, 1), ("x", 1, 3, 0),
    ("z", 1, 3, 0, 0), ("z", 0, 2, 0, 1), ("z", 1, 3, 1, 0), ("P", 1), ("Q", 1), ("z", 0, 2, 0, 3), ("z", 0, 2, 1, 2),
    ("z", 0, 2, 1, 1), ("z", 0, 2, 0, 2), ("P", 2), ("S2", 1), ("Q", 2), ("z", 0, 3, 0, 0), ("z", 0, 2, 1, 3),
    ("x", 1, 4, 0), ("S2", 2), ("z", 0, 3, 1, 0), ("z", 0, 3, 0, 1), ("z", 0, 3, 1, 2), ("z", 0, 3, 1, 1),
    ("f", 1, 3, 1, 2), ("z", 0, 3, 0, 3), ("z", 0, 3, 0, 2), ("f", 1, 3, 1, 1), ("f", 1, 3, 0, 2), ("z", 0, 3, 1, 3),
    ("f", 1, 3, 0, 1), ("S3", 1, 0), ("S3", 1, 1), ("S3", 2, 0), ("P", 4), ("Q", 4), ("P", 3), ("Q", 3), ("S4", 1, 0),
    ("S3", 2, 1), ("S4", 1, 1), ("S2", 3), ("S5", 1, 0), ("S4", 2, 0), ("S3", 4, 0), ("S5", 1, 1), ("S5", 2, 0),
    ("S4", 2, 1), ("S3", 3, 0), ("S3", 3, 1), ("S5", 2, 1), ("S3", 0, 0), ("S6", 1, 0), ("S5", 4, 0), ("S4", 3, 0),
    ("S6", 1, 1), ("S4", 3, 1), ("S5", 3, 0), ("S4", 0, 0), ("S6", 2, 1), ("S6", 2, 0), ("S5", 3, 1), ("S5", 0, 0),
    ("W", 1, 0), ("S6", 4, 0), ("W", 0, 0), ("W", 1, 1), ("S6", 3, 0), ("S6", 3, 1), ("W", 0, 1), ("E1",),
    ("S6", 0, 0), ("E3",), ("E2",),
)


def ways(s):
    return (0, 1) if s in (1, 2, 3) else (0,)


def block(s, d, f):
    return GROUPS[s][0] + 4 * d + f


def gelu_pair(pre_act, back_act):
    coeff = math.sqrt(2.0 / math.pi)
    inner = coeff * (pre_act + 0.044715 * pre_act * pre_act * pre_act)
    tanh_val = jnp.tanh(inner)
    activated = (0.5 * pre_act * (1.0 + tanh_val)).astype(BF16)
    slope = 0.5 * (1.0 + tanh_val) + 0.5 * pre_act * (1.0 - tanh_val * tanh_val) * coeff * (
        1.0 + 3.0 * 0.044715 * pre_act * pre_act
    )
    return activated, (back_act * slope).astype(BF16)


def dot(a, b, dims):
    return lax.dot_general(a, b, ((dims[:1], dims[1:]), ((), ())), preferred_element_type=F32)


def kernel(
    tok_hbm, grad_hbm, win_hbm, wout_hbm, GIN, GW1, GW2,
    X, W1, W2, W1T, W2T, KS, KO, KR, C, R, R8, H, G, RA, RM, SA, RX, RB, SB, HOLD, RZ, RN, OUT,
    local_sem, sent,
    a_recv, b_recv, k_recv, r_recv, r8_recv, y_recv, h_recv, ra_recv, rb_recv, rx_recv, rz_recv,
):
    row, col = lax.axis_index("row"), lax.axis_index("col")
    y, core, z, x = row // 2, row % 2, col // 4, col % 4

    def at(dz=0, dx=0, dy=0, other=False):
        return {
            "row": lax.rem(y + dy + 4, 4) * 2 + (1 - core if other else core),
            "col": lax.rem(z + dz + 8, 8) * 4 + lax.rem(x + dx + 4, 4),
        }

    mine = pl.multiple_of(core * HALF, HALF)
    theirs = pl.multiple_of((1 - core) * HALF, HALF)
    local = [
        pltpu.make_async_copy(tok_hbm, X.at[0, pl.ds(0, ROWS)], local_sem.at[0]),
        pltpu.make_async_copy(grad_hbm, X.at[1, pl.ds(0, ROWS)], local_sem.at[1]),
        pltpu.make_async_copy(win_hbm.at[:, pl.ds(mine, HALF)], W1.at[:, pl.ds(0, HALF)], local_sem.at[2]),
        pltpu.make_async_copy(win_hbm.at[:, pl.ds(theirs, HALF)], W1.at[:, pl.ds(HALF, HALF)], local_sem.at[3]),
        pltpu.make_async_copy(wout_hbm.at[pl.ds(mine, HALF)], W2.at[pl.ds(0, HALF)], local_sem.at[4]),
        pltpu.make_async_copy(wout_hbm.at[pl.ds(theirs, HALF)], W2.at[pl.ds(HALF, HALF)], local_sem.at[5]),
    ]
    for copy in local:
        copy.start()

    partners = [at(dz=i) for i in range(1, 8)] + [at(dx=i) for i in range(1, 4)] + [at(dy=i) for i in range(1, 4)]
    partners += [at(dy=i, other=True) for i in range(4)]
    barrier = pltpu.get_barrier_semaphore()
    for partner in partners:
        pl.semaphore_signal(barrier, inc=1, device_id=partner, device_id_type=MESH)
    pl.semaphore_wait(barrier, len(partners))

    done = set()

    def once(key):
        new = key not in done
        done.add(key)
        return new

    def remote(src, dst, kind, recv, target):
        return pltpu.make_async_remote_copy(
            src_ref=src, dst_ref=dst, send_sem=sent.at[kind], recv_sem=recv, device_id=target, device_id_type=MESH
        )

    def piece(part, s, d, f, which):
        array = pl.ds(0, 2) if which is None else pl.ds(which, 1)
        columns = pl.ds(0, CA) if part == 0 else pl.ds(CA, D - CA)
        return X.at[array, pl.ds(ROWS * block(s, d, f), ROWS), columns]

    def gather(part, src, dst, target, which=None):
        recv = (a_recv, b_recv)[part].at[block(*dst)]
        return remote(piece(part, *src, which), piece(part, *dst, which), part, recv, target)

    def arrived(part, s, d, f):
        if s == f == 0:
            if once("own"):
                local[0].wait()
                local[1].wait()
        elif once((part, s, d, f)):
            gather(part, (s, d, f), (s, d, f), at(dz=1)).wait_recv()

    def along_z(part, s, d, f):
        arrived(part, s, d, f)
        if s == 0:
            gather(part, (0, 0, f), (1, 0, f), at(dz=1)).start()
            gather(part, (0, 0, f), (1, 1, f), at(dz=-1)).start()
        elif s < 3:
            gather(part, (s, d, f), (s + 1, d, f), at(dz=-1 if d else 1)).start()
        else:
            gather(part, (3, d, f), (4, 0, f), at(dz=-1 if d else 1), d).start()

    def along_x(part, s, d):
        arrived(part, s, d, 0)
        gather(part, (s, d, 0), (s, d, 2), at(dx=1)).start()
        gather(part, (s, d, 0), (s, d, 1), at(dx=-1)).start()
        if part == 1 and s in DIRECT:
            gather(part, (s, d, 0), (s, d, 3), at(dx=2)).start()

    def further_x(part, s, d, f):
        arrived(part, s, d, f)
        gather(part, (s, d, f), (s, d, 3), at(dx=-1 if f == 1 else 1), f - 1).start()

    def weights(i):
        if once(("weights", i)):
            local[2 * i].wait()
            local[2 * i + 1].wait()

    def turn(i, j):
        weights(i)
        part = pl.ds(256 * j, 256)
        if i == 1:
            W1T[:, part] = W1[part, :].T
        else:
            W2T[:, part] = W2[part, :].T

    def rows(s):
        return ROWS * GROUPS[s][0], ROWS * GROUPS[s][1]

    def swap_copy(s, i):
        first, n = rows(s)
        part = pl.ds(first, n)
        return remote(KS.at[i, part], KR.at[i, part], 2, k_recv.at[s, i], at(other=True))

    def product(s, i):
        first, n = rows(s)
        part = pl.ds(first, n)
        total = dot(X[i, part, :], (W1, W2T)[i][...], (1, 0))
        KS[i, part, :] = total[:, HALF:].astype(BF16)
        if s == 4:
            C[i, part, :] = total[:, :HALF].astype(BF16)
        else:
            KO[i, part, :] = total[:, :HALF]
            swap_copy(s, i).start()

    def p(s):
        for d in ways(s):
            for f in range(4):
                arrived(0, s, d, f)
                arrived(1, s, d, f)
        weights(1)
        product(s, 0)

    def q(s):
        product(s, 1)
        if s == 4:
            cross_sum(2).start()
            for dy in (2, 1, 3):
                sum_copy(s, 0, dy).start()
            for dy in (1, 3, 0):
                cross_sum(dy).start()

    def first(s, d):
        return ROWS * block(s, d, 0)

    def quarter(s, d, i):
        return pl.ds(pl.multiple_of(first(s, d) + i * ROWS, ROWS), ROWS)

    def sum_copy(s, d, dy):
        there = R.at[dy - 1, :, pl.ds(first(s, d) // 4, ROWS)]
        return remote(C.at[:, quarter(s, d, lax.rem(y + dy, 4))], there, 3, r_recv.at[2 * s + d], at(dy=dy))

    def cross_sum(dy):
        src = KS.at[:, quarter(4, 0, lax.rem(y + dy, 4))]
        return remote(src, R8.at[dy], 2, r8_recv, at(dy=dy, other=True))

    def cross_part(dy):
        where = quarter(4, 0, y)
        there = H.at[:, where, pl.ds(HALF, HALF)]
        return remote(H.at[:, where, pl.ds(0, HALF)], there, 5, h_recv.at[8], at(dy=dy, other=True))

    def s2(s):
        part = pl.ds(*rows(s))
        swap_copy(s, 0).wait_recv()
        swap_copy(s, 1).wait_recv()
        C[:, part, :] = (KO[:, part, :] + KR[:, part, :].astype(F32)).astype(BF16)
        for d in ways(s):
            for dy in (2, 1, 3):
                sum_copy(s, d, dy).start()

    def part_copy(s, d, dy):
        where = H.at[:, quarter(s, d, y), pl.ds(0, HALF)]
        return remote(where, where, 4, y_recv.at[2 * s + d], at(dy=dy))

    def s3(s, d):
        part = pl.ds(first(s, d) // 4, ROWS)
        landed = R.at[:, :, part]
        remote(landed, landed, 3, r_recv.at[2 * s + d], at(dy=1)).wait_recv()
        total = C[:, quarter(s, d, y), :].astype(F32)
        for i in range(3):
            total += R[i, :, part, :].astype(F32)
        if s == 4:
            remote(R8, R8, 2, r8_recv, at(other=True)).wait_recv()
            for i in range(4):
                total += R8[i].astype(F32)
        activated, grad_pre = gelu_pair(total[0], total[1])
        H[0, quarter(s, d, y), 0:HALF] = activated
        H[1, quarter(s, d, y), 0:HALF] = grad_pre
        if s == 4:
            cross_part(2).start()
        for dy in (2, 1, 3):
            part_copy(s, d, dy).start()
        if s == 4:
            for dy in (1, 3, 0):
                cross_part(dy).start()

    def half_copy(s, d):
        part = pl.ds(first(s, d), 4 * ROWS)
        there = H.at[:, part, pl.ds(HALF, HALF)]
        return remote(H.at[:, part, pl.ds(0, HALF)], there, 5, h_recv.at[2 * s + d], at(other=True))

    def quarters(s, d):
        landed = H.at[:, pl.ds(first(s, d), 3 * ROWS), pl.ds(0, HALF)]
        remote(landed, landed, 4, y_recv.at[2 * s + d], at(dy=1)).wait_recv()

    def s4(s, d):
        quarters(s, d)
        half_copy(s, d).start()

    def z_copy(src, s, d, kind, recv, straight, added):
        if MERGE and s == 3:
            return remote(src, added.at[d], kind, recv.at[1 + d], at(dz=1 if d else -1))
        return remote(src, straight.at[ZSLOT[s] + d], kind, recv.at[0], at(dz=s if d else -s))

    def ra_copy(s, d):
        return z_copy(G.at[pl.ds(first(s, d), 4 * ROWS), pl.ds(0, ZA)], s, d, 6, ra_recv, RA, RM)

    def rb_copy(s, d, f):
        i = 2 * s + d
        src = G.at[pl.ds(ROWS * block(s, d, f), ROWS), pl.ds(ZA, ZB)]
        return remote(src, RB.at[i, f - 1], 7, rb_recv.at[i], at(dx=XOFF[f]))

    def rz_copy(s, d):
        return z_copy(SB.at[2 * (s - 1) + d], s, d, 8, rz_recv, RZ, RN)

    def rx_copy(f):
        src = SA.at[pl.ds(ROWS * f, ROWS)]
        return remote(src, RX.at[f - 1], 9, rx_recv, at(dx=XOFF[f]))

    def s5(s, d):
        if s == 4:
            quarters(s, d)
        half_copy(s, d).wait_recv()
        part = pl.ds(first(s, d), 4 * ROWS)
        G[part, :] = dot(H[1, part, :], W1T[...], (1, 0)).astype(BF16)
        for f in (3, 1, 2):
            rb_copy(s, d, f).start()
        if s and not (MERGE and s == 2):
            ra_copy(s, d).start()

    def ma(d):
        remote(RM.at[d], RM.at[d], 6, ra_recv.at[1 + d], at(dz=1)).wait_recv()
        part = pl.ds(first(2, d), 4 * ROWS)
        G[part, pl.ds(0, ZA)] = (G[part, pl.ds(0, ZA)].astype(F32) + RM[d].astype(F32)).astype(BF16)
        ra_copy(2, d).start()

    def s6(s, d):
        i = 2 * s + d
        remote(RB.at[i], RB.at[i], 7, rb_recv.at[i], at(dx=1)).wait_recv()
        total = G[pl.ds(first(s, d), ROWS), pl.ds(ZA, ZB)].astype(F32)
        for j in range(3):
            total += RB[i, j].astype(F32)
        if s == 0:
            OUT[:, pl.ds(ZA, ZB)] = total
        elif MERGE and s == 2:
            HOLD[d] = total
        else:
            SB[2 * (s - 1) + d] = total.astype(BF16)
            rz_copy(s, d).start()

    def mz(d):
        remote(RN.at[d], RN.at[d], 8, rz_recv.at[1 + d], at(dz=1)).wait_recv()
        SB[2 + d] = (HOLD[d] + RN[d].astype(F32)).astype(BF16)
        rz_copy(2, d).start()

    def w(i, j):
        if i == 0:
            part = pl.ds(j * (D // 2), D // 2)
            total = dot(X[0, :, part], H[1], (0, 0)).astype(BF16)
            GW1[part, pl.ds(mine, HALF)] = total[:, :HALF]
            GW1[part, pl.ds(theirs, HALF)] = total[:, HALF:]
        else:
            total = dot(H[0, :, pl.ds(j * HALF, HALF)], X[1], (0, 0)).astype(BF16)
            GW2[pl.ds(theirs if j else mine, HALF), :] = total

    def e1():
        remote(RA, RA, 6, ra_recv.at[0], at(dz=1)).wait_recv()
        total = G[pl.ds(0, 4 * ROWS), pl.ds(0, ZA)].astype(F32)
        for i in range(ZSUMS):
            total += RA[i].astype(F32)
        OUT[:, pl.ds(0, ZA)] = total[:ROWS]
        SA[...] = total.astype(BF16)
        for f in (3, 1, 2):
            rx_copy(f).start()

    def e2():
        remote(RZ, RZ, 8, rz_recv.at[0], at(dz=1)).wait_recv()
        total = OUT[:, pl.ds(ZA, ZB)]
        for i in range(ZSUMS):
            total += RZ[i].astype(F32)
        GIN[:, pl.ds(ZA, ZB)] = total.astype(BF16)

    def e3():
        remote(RX, RX, 9, rx_recv, at(dx=1)).wait_recv()
        total = OUT[:, pl.ds(0, ZA)]
        for i in range(3):
            total += RX[i].astype(F32)
        GIN[:, pl.ds(0, ZA)] = total.astype(BF16)

    steps = {
        "z": along_z, "x": along_x, "f": further_x, "T": turn, "P": p, "Q": q, "S2": s2, "S3": s3, "S4": s4, "S5": s5,
        "S6": s6, "MA": ma, "MZ": mz, "W": w, "E1": e1, "E2": e2, "E3": e3,
    }
    for name, *args in ORDER:
        steps[name](*args)
    moved = 31 * ROWS
    for kind, ref in enumerate((
        X.at[:, pl.ds(0, moved), pl.ds(0, CA)],
        X.at[:, pl.ds(0, moved), pl.ds(CA, D - CA)],
        KS,
        C.at[:, pl.ds(0, 3 * TOK // 4)],
        H.at[:, pl.ds(0, 3 * TOK // 4), pl.ds(0, HALF)],
        H.at[:, :, pl.ds(0, HALF)],
        G.at[pl.ds(0, 28 * ROWS), pl.ds(0, ZA)],
        G.at[pl.ds(0, 24 * ROWS), pl.ds(ZA, ZB)],
        SB,
        RX,
    )):
        remote(ref, ref, kind, rx_recv, at(dz=1)).wait_send()


def write_out(a, b, c, a_hbm, b_hbm, c_hbm, sem):
    copies = [pltpu.make_async_copy(a, a_hbm, sem.at[0])]
    for i, (src, dst) in enumerate(((b, b_hbm), (c, c_hbm))):
        n = src.shape[0] // 2
        for j in range(2):
            part = pl.ds(j * n, n)
            copies.append(pltpu.make_async_copy(src.at[part], dst.at[part], sem.at[1 + 2 * i + j]))
    for copy in copies:
        copy.start()
    for copy in copies:
        copy.wait()


def per_device(tokens, grad_out, w_in, w_out):
    hbm, vmem = pl.BlockSpec(memory_space=pltpu.HBM), pl.BlockSpec(memory_space=pltpu.VMEM)
    dma = pltpu.SemaphoreType.DMA
    scratch = [
        pltpu.VMEM((2, TOK, D), BF16),
        pltpu.VMEM((D, FF), BF16),
        pltpu.VMEM((FF, D), BF16),
        pltpu.VMEM((FF, D), BF16),
        pltpu.VMEM((D, FF), BF16),
        pltpu.VMEM((2, TOK, HALF), BF16),
        pltpu.VMEM((2, TOK, HALF), F32),
        pltpu.VMEM((2, TOK, HALF), BF16),
        pltpu.VMEM((2, TOK, HALF), BF16),
        pltpu.VMEM((3, 2, TOK // 4, HALF), BF16),
        pltpu.VMEM((4, 2, ROWS, HALF), BF16),
        pltpu.VMEM((2, TOK, FF), BF16),
        pltpu.VMEM((TOK, D), BF16),
        pltpu.VMEM((ZSUMS, 4 * ROWS, ZA), BF16),
        pltpu.VMEM((2, 4 * ROWS, ZA), BF16),
        pltpu.VMEM((4 * ROWS, ZA), BF16),
        pltpu.VMEM((3, ROWS, ZA), BF16),
        pltpu.VMEM((9, 3, ROWS, ZB), BF16),
        pltpu.VMEM((7, ROWS, ZB), BF16),
        pltpu.VMEM((2, ROWS, ZB), F32),
        pltpu.VMEM((ZSUMS, ROWS, ZB), BF16),
        pltpu.VMEM((2, ROWS, ZB), BF16),
        pltpu.VMEM((ROWS, D), F32),
        dma((6,)),
        dma((10,)),
    ]
    for shape in ((32,), (32,), (5, 2), (9,), (), (9,), (9,), (3,), (9,), (), (3,)):
        scratch.append(dma(shape))
    results = (
        jax.ShapeDtypeStruct((ROWS, D), BF16),
        jax.ShapeDtypeStruct((D, FF), BF16),
        jax.ShapeDtypeStruct((FF, D), BF16),
    )
    held = pl.pallas_call(
        kernel,
        out_shape=tuple(pltpu.VMEM(r.shape, r.dtype) for r in results),
        in_specs=[hbm] * 4,
        out_specs=(vmem, vmem, vmem),
        scratch_shapes=scratch,
        compiler_params=pltpu.CompilerParams(collective_id=0, has_side_effects=True, vmem_limit_bytes=40 * 2**20),
        cost_estimate=pl.CostEstimate(flops=10 * TOK * D * FF, bytes_accessed=8 * D * FF, transcendentals=TOK * HALF // 4),
    )(*(pltpu.with_memory_space_constraint(arg, pltpu.HBM) for arg in (tokens, grad_out, w_in, w_out)))
    return pl.pallas_call(
        write_out,
        out_shape=tuple(pltpu.HBM(r.shape, r.dtype) for r in results),
        in_specs=[vmem] * 3,
        out_specs=(hbm, hbm, hbm),
        scratch_shapes=[dma((5,))],
        compiler_params=pltpu.CompilerParams(vmem_limit_bytes=8 * 2**20),
        cost_estimate=pl.CostEstimate(flops=0, bytes_accessed=8 * D * FF, transcendentals=0),
    )(*(pltpu.with_memory_space_constraint(array, pltpu.VMEM) for array in held))


def solution(mesh):
    return jax.shard_map(
        per_device,
        mesh=mesh,
        in_specs=(P("col", "row"), P("col", "row"), P("row", "col"), P("col", "row")),
        out_specs=(P("col", "row"), P("row", "col"), P("col", "row")),
        check_vma=False,
    )
```
